32 devices in a mesh: dp: 8 (over z, x), tensor: 4 (over y, core).
Axes of the slice: x: 2, y: 2, z: 4, core: 2. Of those that a mesh axis runs over, the one named last changes fastest.
Arguments:
- tokens: bfloat16 [8, 1024, 768], P('dp'), may hold values from -6 to 6
- cotangent: bfloat16 [8, 1024, 768], P('dp'), may hold values from -6 to 6
- tie: int32 [12], replicated, may hold values 0 or 1
- ln1_gain: float32 [2, 768], replicated, may hold values from 0.5 to 1.5
- ln1_shift: float32 [2, 768], replicated, may hold values from -1 to 1
- w_qkv: bfloat16 [2, 768, 3, 768], P(None, None, None, 'tensor'), may hold values from -0.21875 to 0.21875
- b_qv: float32 [2, 2, 768], P(None, None, 'tensor'), may hold values from -1 to 1
- w_proj: bfloat16 [2, 768, 768], P(None, 'tensor'), may hold values from -1.25 to 1.25
- b_proj: float32 [2, 768], replicated, may hold values from -1 to 1
- ln2_gain: float32 [2, 768], replicated, may hold values from 0.5 to 1.5
- ln2_shift: float32 [2, 768], replicated, may hold values from -1 to 1
- w_fc: bfloat16 [2, 768, 3072], P(None, None, 'tensor'), may hold values from -0.21875 to 0.21875
- b_fc: float32 [2, 3072], P(None, 'tensor'), may hold values from -1 to 1
- w_out: bfloat16 [2, 3072, 768], P(None, 'tensor'), may hold values from -0.109375 to 0.109375
- b_out: float32 [2, 768], replicated, may hold values from -1 to 1
Outputs:
- output: bfloat16 [8, 1024, 768], P('dp')
- grad_tokens: float32 [8, 1024, 768], P('dp')
- grad_ln1_gain: float32 [2, 768], P(None, 'dp')
- grad_ln1_shift: float32 [2, 768], P(None, 'dp')
- grad_w_qkv: float32 [2, 768, 3, 768], P(None, 'dp', None, 'tensor')
- grad_b_qv: float32 [2, 2, 768], P(None, None, ('tensor', 'dp'))
- grad_w_proj: float32 [2, 768, 768], P(None, 'tensor', 'dp')
- grad_b_proj: float32 [2, 768], P(None, 'dp')
- grad_ln2_gain: float32 [2, 768], P(None, 'dp')
- grad_ln2_shift: float32 [2, 768], P(None, 'dp')
- grad_w_fc: float32 [2, 768, 3072], P(None, 'dp', 'tensor')
- grad_b_fc: float32 [2, 3072], P(None, ('tensor', 'dp'))
- grad_w_out: float32 [2, 3072, 768], P(None, 'tensor', 'dp')
- grad_b_out: float32 [2, 768], P(None, 'dp')
The draws below stay inside these ranges and needn't reach their ends.
Inputs may be any that keep to these rules, and one draw needn't show every extreme that they name: tie[i] refers to the i-th weight argument in the order ln1_gain, ln1_shift, w_qkv, b_qv, w_proj, b_proj, ln2_gain, ln2_shift, w_fc, b_fc, w_out, b_out.
All inputs are finite; a program needn't handle non-finite values.
Results may differ from the reference program's by a relative error of at most 0.028.
Values may be sent and summed in bfloat16 or wider, within the bound.
No kernel may reach another device: no remote copies, remote signals or barrier semaphores. Data moves between devices by JAX's collectives and lax.ppermute only.
A program may use at most 192 MiB of HBM per device.

```python
import jax
import jax.numpy as jnp
from jax import lax

D = 768
HEADS = 12
HEAD = 64
FF = 3072
SEQ_LEN = 1024
SEQS = 8
N_TENSOR = 4


def touch_ends(values, rng, least, largest):
    place = [jax.random.randint(jax.random.fold_in(rng, axis), (), 0, length) for axis, length in enumerate(values.shape)]
    widest = values.shape.index(max(values.shape))
    next_to = place[:widest] + [(place[widest] + 1) % values.shape[widest]] + place[widest + 1:]
    return values.at[tuple(place)].set(least).at[tuple(next_to)].set(largest)


def shard_levels(stream_key, shape, pieces, least, high):
    loudness, own = 1.0, jax.random.fold_in(stream_key, 6)
    for dim, shards_of in pieces:
        draws = jnp.exp(jax.random.uniform(jax.random.fold_in(own, dim), (shards_of,), jnp.float32, least / len(pieces), high / len(pieces)))
        loudness = loudness * jnp.repeat(draws, shape[dim] // shards_of).reshape([-1 if axis == dim else 1 for axis in range(len(shape))])
    return loudness


def noise(rng, dims, spread, most, pieces=(), dtype=jnp.bfloat16):
    drawn = jax.random.normal(rng, dims, jnp.float32) * spread
    if len(pieces) > 0:
        drawn = shard_levels(rng, dims, pieces, -0.22, 0.18) * drawn
    return jnp.clip(drawn, min=-most, max=most).astype(dtype)


def setup_inputs(seed: int = 0) -> dict:
    key_of = jax.random.split(jax.random.key(seed), 16)
    return {
        "tokens": noise(key_of[0], (SEQS, SEQ_LEN, D), 1.0, 6.0, ((0, 8),)),
        "cotangent": noise(key_of[1], (SEQS, SEQ_LEN, D), 1.0, 6.0, ((0, 8),)),
        "tie": touch_ends((jax.random.randint(key_of[2], (12,), 0, 2) < 1).astype(jnp.int32), jax.random.fold_in(key_of[2], 1), 0, 1),
        "ln1_gain": jnp.clip(1.0 + 0.1 * jax.random.normal(key_of[3], (2, D), jnp.float32), 0.5, 1.5),
        "ln1_shift": noise(key_of[4], (2, D), 0.2, 1.0, (), jnp.float32),
        "w_qkv": noise(key_of[5], (2, D, 3, D), D ** -0.5, 0.21875, ((3, 4),)),
        "b_qv": noise(key_of[6], (2, 2, D), 0.2, 1.0, ((2, 4),), jnp.float32),
        "w_proj": noise(key_of[7], (2, D, D), (D // 32) ** -0.5, 1.25, ((1, 4),)),
        "b_proj": noise(key_of[8], (2, D), 0.2, 1.0, (), jnp.float32),
        "ln2_gain": jnp.clip(1.0 + 0.1 * jax.random.normal(key_of[9], (2, D), jnp.float32), 0.5, 1.5),
        "ln2_shift": noise(key_of[10], (2, D), 0.2, 1.0, (), jnp.float32),
        "w_fc": noise(key_of[11], (2, D, FF), D ** -0.5, 0.21875, ((2, 4),)),
        "b_fc": noise(key_of[12], (2, FF), 0.2, 1.0, ((1, 4),), jnp.float32),
        "w_out": noise(key_of[13], (2, FF, D), FF ** -0.5, 0.109375, ((1, 4),)),
        "b_out": noise(key_of[14], (2, D), 0.2, 1.0, (), jnp.float32),
    }


EPS = 1e-05
NEG = -1e+30
HIGH = lax.Precision.HIGHEST

@jax.custom_vjp
def low(v):
    return lax.optimization_barrier(v.astype(jnp.bfloat16)).astype(jnp.float32)

@jax.custom_vjp
def low_back(v):
    return v

def low_keep(v):
    return (low(v), None)

def low_pass(kept, grad):
    return (grad,)

def back_keep(v):
    return (v, None)

def back_low(kept, grad):
    return (low(grad),)
low.defvjp(low_keep, low_pass)
low_back.defvjp(back_keep, back_low)

def norm_rows(value, gain, shift):
    center = value - lax.optimization_barrier(jnp.mean(value, axis=-1, keepdims=True))
    scale = lax.rsqrt(lax.optimization_barrier(jnp.mean(center * center, axis=-1, keepdims=True)) + EPS)
    return center * scale * gain + shift

def product(left, right):
    return jnp.dot(left, right, precision=HIGH)

def rounded_both(value):
    return low(low_back(value))

def split_sum(left, right):
    width = left.shape[1] // N_TENSOR
    total = jnp.zeros((left.shape[0], right.shape[1]), jnp.float32)
    for group in range(N_TENSOR):
        total = total + low(product(left[:, group * width:(group + 1) * width], right[group * width:(group + 1) * width]))
    return low_back(total)

def block_forward(hidden, weights):
    gain_one, shift_one, w_qkv, b_qv, w_proj, b_proj, gain_two, shift_two, w_fc, b_fc, w_out, b_out = weights
    length = hidden.shape[0]
    scale = HEAD ** (-0.5)
    normed = low(norm_rows(hidden, gain_one, shift_one))
    queries = rounded_both(product(normed, w_qkv[:, 0]) + b_qv[0])
    keys = rounded_both(product(normed, w_qkv[:, 1]))
    values = rounded_both(product(normed, w_qkv[:, 2]) + b_qv[1])
    query_heads = queries.reshape(length, HEADS, HEAD)
    key_heads = keys.reshape(length, HEADS, HEAD)
    value_heads = values.reshape(length, HEADS, HEAD)
    scores = low_back(jnp.einsum('qhd,khd->hqk', query_heads, key_heads, precision=HIGH) * scale)
    allowed = jnp.arange(length)[:, None] >= jnp.arange(length)[None, :]
    scores = jnp.where(allowed[None], scores, NEG)
    peak = lax.optimization_barrier(jnp.max(scores, axis=-1, keepdims=True))
    powers = jnp.exp(scores - peak)
    probs = low(powers / lax.optimization_barrier(jnp.sum(powers, axis=-1, keepdims=True)))
    context = rounded_both(jnp.einsum('hqk,khd->qhd', probs, value_heads, precision=HIGH).reshape(length, HEADS * HEAD))
    middle = hidden + split_sum(context, w_proj) + b_proj
    mixed = low(norm_rows(middle, gain_two, shift_two))
    before = low_back(product(mixed, w_fc) + b_fc)
    active = low(jax.nn.gelu(before, approximate=True))
    return middle + split_sum(active, w_out) + b_out

def reference(tokens, cotangent, tie, ln1_gain, ln1_shift, w_qkv, b_qv, w_proj, b_proj, ln2_gain, ln2_shift, w_fc, b_fc, w_out, b_out):
    stacks = tuple((array.astype(jnp.float32) for array in (ln1_gain, ln1_shift, w_qkv, b_qv, w_proj, b_proj, ln2_gain, ln2_shift, w_fc, b_fc, w_out, b_out)))

    def forward(hidden, weights):
        first = tuple((stack[0] for stack in weights))
        second = tuple((jnp.where(tie[index] == 1, weights[index][0], weights[index][1]) for index in range(12)))
        return block_forward(block_forward(hidden, first), second)

    def one(carry, pair):
        seq_tokens, seq_grad = pair
        result, pull = jax.vjp(forward, seq_tokens.astype(jnp.float32), stacks)
        grad_input, grad_weights = pull(seq_grad.astype(jnp.float32))
        return (tuple((total + grad for total, grad in zip(carry, grad_weights))), (result.astype(jnp.bfloat16), grad_input))
    zeros = tuple((jnp.zeros_like(stack) for stack in stacks))
    totals, (outputs, grad_inputs) = lax.scan(one, zeros, (tokens, cotangent))
    return (outputs, grad_inputs, totals[0], totals[1], totals[2], totals[3], totals[4], totals[5], totals[6], totals[7], totals[8], totals[9], totals[10], totals[11])
```

```python
import functools

import jax
import jax.numpy as jnp
from jax import lax
from jax.experimental import pallas as pl
from jax.experimental.pallas import tpu as pltpu
from jax.sharding import PartitionSpec as P

HEAD = 64
LANES = 128
EPS = 1e-05
NEG = -1e30
BF = jnp.bfloat16
F32 = jnp.float32
SDS = jax.ShapeDtypeStruct
GELU_C = 0.7978845608028654
GELU_A = 0.044715
LIMIT = 5
COST = 0.5
CHUNKS = 4

(LN1_GAIN, LN1_SHIFT, W_QKV, B_QV, W_PROJ, B_PROJ, LN2_GAIN, LN2_SHIFT, W_FC, B_FC, W_OUT, B_OUT, CORE, PLACE, CHIP) = range(15)


def dot_nn(a, b):
    return lax.dot_general(a, b, (((1,), (0,)), ((), ())), preferred_element_type=F32)


def dot_nt(a, b):
    return lax.dot_general(a, b, (((1,), (1,)), ((), ())), preferred_element_type=F32)


def stats(v):
    center = v - jnp.mean(v, axis=-1, keepdims=True)
    r = lax.rsqrt(jnp.mean(center * center, axis=-1, keepdims=True) + EPS)
    return center * r, r


def norm(v, gain, shift):
    return stats(v)[0] * gain + shift


def norm_back(v, gain, grad):
    xhat, r = stats(v)
    e = grad * gain
    back = r * (e - jnp.mean(e, axis=-1, keepdims=True) - xhat * jnp.mean(e * xhat, axis=-1, keepdims=True))
    return back, jnp.sum(grad * xhat, axis=0, keepdims=True), jnp.sum(grad, axis=0, keepdims=True)


def pair_sum(own, other):
    return own.astype(F32) + other.astype(F32)


def copy_of(meta, layer, index):
    return 0 if layer == 0 else 1 - meta[index]


def vector(ref, meta, layer, index):
    return ref[pl.ds(copy_of(meta, layer, index), 1), :]


class Order:
    def __init__(self):
        self.waits = []

    def take(self):
        found, self.waits = self.waits, []
        return found

    def done(self, token):
        self.waits.append(token)


def call(order, body, outs, scratch, args, micros, limit=LIMIT, keep=True):
    deps = order.take()
    count, gap = len(args), len(deps)

    def run(*refs):
        token = count + gap + len(outs)
        refs[token][...] = jnp.zeros_like(refs[token])
        body(*refs[:count], *refs[count + gap:token], *refs[token + 1:])

    vmem = pl.BlockSpec(memory_space=pltpu.VMEM)
    found = pl.pallas_call(
        run,
        in_specs=[pl.BlockSpec(memory_space=pltpu.SMEM)] + [vmem] * (count - 1)
        + [pl.BlockSpec(memory_space=pl.ANY)] * gap,
        out_specs=[vmem] * (len(outs) + 1),
        out_shape=([pltpu.VMEM(o.shape, o.dtype) for o in outs] if keep else list(outs)) + [pltpu.VMEM((8, LANES), F32)],
        scratch_shapes=scratch,
        compiler_params=pltpu.CompilerParams(vmem_limit_bytes=limit * 2 ** 20),
        cost_estimate=pl.CostEstimate(flops=int(micros * COST * 1.15e9), bytes_accessed=1024, transcendentals=0),
    )(args[0], *[pltpu.with_memory_space_constraint(a, pltpu.VMEM) for a in args[1:]], *deps)
    *found, token = found
    order.done(token)
    return found


def tiles(total, size):
    return [slice(at, min(at + size, total)) for at in range(0, total, size)]


def pair_loop(width, body):
    def step(j, carry):
        body(j, pl.ds(pl.multiple_of(j * LANES, LANES), LANES))
        return carry
    lax.fori_loop(0, width // LANES, step, 0)


def prep_body(layer, meta, w_own, w_sib, p_own, p_sib, qkv, proj):
    half = p_own.shape[1]
    c_w, c_p = copy_of(meta, layer, W_QKV), copy_of(meta, layer, W_PROJ)
    for core, (own, other) in enumerate(((slice(0, half), slice(half, 2 * half)), (slice(half, 2 * half), slice(0, half)))):
        @pl.when(meta[CORE] == core)
        def _():
            qkv[:, own, :] = w_own[c_w]
            qkv[:, other, :] = w_sib[c_w]
            proj[own, :] = p_own[c_p]
            proj[other, :] = p_sib[c_p]


def prep(order, layer, meta, w, p):
    _, three, half, model = w[0].shape
    outs = [SDS((three, 2 * half, model), BF), SDS((2 * half, model), BF)]
    return call(order, functools.partial(prep_body, layer), outs, [], (meta, *w, *p), 0.8)


def prep_whole_body(layer, meta, *refs):
    *parts, proj = refs
    half = parts[0].shape[1]
    copy = copy_of(meta, layer, W_PROJ)
    own, sibling, far = parts[0], parts[1], parts[2:]
    for me in range(4):
        @pl.when((meta[CORE] == me % 2) & (meta[CHIP] == me // 2))
        def _():
            for part, place in ((own, me), (sibling, me ^ 1)):
                proj[place * half:(place + 1) * half, :] = part[copy]
            for i, place in enumerate((me ^ 2, me ^ 3)):
                rows = slice(place * half, (place + 1) * half)
                if layer == 0:
                    proj[rows, :] = far[i][...]
                else:
                    proj[rows, :] = jnp.where(copy == 0, far[2 * i][...], far[2 * i + 1][...])


def prep_whole(order, layer, meta, near, far):
    _, half, model = near[0].shape
    far = [v for pair in far for v in pair[:layer + 1]]
    return call(order, functools.partial(prep_whole_body, layer), [SDS((4 * half, model), BF)], [],
                (meta, *near, *far), 0.7)[0]


def attn_in_body(layer, meta, *refs):
    if layer == 0:
        x_ref, *refs = refs
        gain, shift, w, b_own, b_sib, normed, q, kv = refs
        x = x_ref[...].astype(F32)
    else:
        mid, own, other, b_out, *refs = refs
        gain, shift, w, b_own, b_sib, hid, normed, q, kv = refs
        x = mid[...] + pair_sum(own[...], other[...]) + vector(b_out, meta, layer - 1, B_OUT)
        hid[...] = x
    normed[...] = norm(x, vector(gain, meta, layer, LN1_GAIN), vector(shift, meta, layer, LN1_SHIFT)).astype(BF)
    core = meta[CORE]
    copy = copy_of(meta, layer, B_QV)

    def bias(i):
        one, two = b_own[copy, i:i + 1, :], b_sib[copy, i:i + 1, :]
        return jnp.concatenate([jnp.where(core == 0, one, two), jnp.where(core == 0, two, one)], axis=1)

    q[...] = (dot_nt(normed[...], w[0]) + bias(0)).astype(BF) * BF(HEAD ** -0.5)
    kv[0] = dot_nt(normed[...], w[1]).astype(BF)
    kv[1] = (dot_nt(normed[...], w[2]) + bias(1)).astype(BF)


def attn_in(order, layer, meta, ins, gain, shift, w, biases):
    n, model = ins[0].shape
    width = w.shape[1]
    outs = [SDS((n, model), F32)] * layer + [SDS((n, model), BF), SDS((n, width), BF), SDS((2, n, width), BF)]
    return call(order, functools.partial(attn_in_body, layer), outs, [],
                (meta, *ins, gain, shift, w, *biases), 1.6)


def head_masks():
    lane = lax.broadcasted_iota(jnp.int32, (1, LANES), 1)
    return [(lane < HEAD), (lane >= HEAD)]


def mask_scores(stream, index, s, core):
    if index == 0:
        keys = lax.broadcasted_iota(jnp.int32, s.shape, 0)
        queries = lax.broadcasted_iota(jnp.int32, s.shape, 1)
        return jnp.where(keys <= queries, s, NEG)
    if index == (1, 3)[stream]:
        return jnp.where(core == (1, 0)[stream], s, NEG)
    return s


def attn_fwd_body(stream, meta, q_ref, *refs):
    count = (2, 4)[stream]
    kvs, (ctx, lse) = refs[:count], refs[count:]
    core = meta[CORE]

    def pair(j, lanes):
        q = q_ref[:, lanes]
        outs = []
        vts = [jnp.transpose(kv[1, :, lanes]) for kv in kvs]
        for h, mask in enumerate(head_masks()):
            qh = jnp.where(mask, q, BF(0))
            s = [mask_scores(stream, i, dot_nt(kv[0, :, lanes], qh), core) for i, kv in enumerate(kvs)]
            peak = functools.reduce(jnp.maximum, [jnp.max(v, axis=0, keepdims=True) for v in s])
            powers = [jnp.exp(v - peak) for v in s]
            total = sum(jnp.sum(v, axis=0, keepdims=True) for v in powers)
            found = sum(dot_nn(vt[h * HEAD:(h + 1) * HEAD], v.astype(BF)) for vt, v in zip(vts, powers))
            outs.append(found / total)
            lse[j, h:h + 1, :] = peak + jnp.log(total)
        ctx[:, lanes] = jnp.transpose(jnp.concatenate(outs, axis=0)).astype(BF)

    pair_loop(q_ref.shape[1], pair)


def attn_fwd(order, stream, meta, q, kvs):
    n, width = q.shape
    outs = [SDS((n, width), BF), SDS((width // LANES, 8, n), F32)]
    return call(order, functools.partial(attn_fwd_body, stream), outs, [], (meta, q, *kvs),
                (3.7, 5.0)[stream])


def mlp_fwd_body(layer, meta, hid, ctx, ctx_peer, proj, b_proj, gain, shift, fc_own, fc_sib, b_own, b_sib, out_own, out_sib,
                 mid, mixed, act, slope, *refs):
    *refs, joined = refs
    term, acc = refs if refs else (None, None)
    width = ctx.shape[1]
    for chip in (0, 1):
        @pl.when(meta[CHIP] == chip)
        def _():
            joined[:, chip * width:(chip + 1) * width] = ctx[...]
            joined[:, (1 - chip) * width:(2 - chip) * width] = ctx_peer[...]
    x = hid[...].astype(F32) + dot_nn(joined[...], proj[...]) + vector(b_proj, meta, layer, B_PROJ)
    mid[...] = x
    mixed[...] = norm(x, vector(gain, meta, layer, LN2_GAIN), vector(shift, meta, layer, LN2_SHIFT)).astype(BF)
    c_fc, c_out = copy_of(meta, layer, W_FC), copy_of(meta, layer, W_OUT)
    for side, (fc, b, out) in enumerate(((fc_own, b_own, out_own), (fc_sib, b_sib, out_sib))):
        bias = vector(b, meta, layer, B_FC)
        for at, cols in enumerate(tiles(fc.shape[2], 256)):
            u = dot_nn(mixed[...], fc[c_fc, :, cols]) + bias[:, cols]
            square = u * u
            t = jnp.tanh(GELU_C * u * (1.0 + GELU_A * square))
            half = 0.5 + 0.5 * t
            active = (u * half).astype(BF)
            act[side, :, cols] = active
            slope[side, :, cols] = (
                half + (0.5 * u) * (1.0 - t * t) * (GELU_C + (3.0 * GELU_A * GELU_C) * square)).astype(BF)
            if term is None:
                continue
            part = dot_nn(active, out[c_out, cols, :])
            if side == 0 and at == 0:
                acc[...] = part
            else:
                acc[...] += part
    if term is not None:
        term[...] = acc[...].astype(BF)


def mlp_fwd(order, layer, meta, hid, attn, vecs, fc, b_fc, out, with_term):
    n, model = hid.shape
    units = fc[0].shape[2]
    outs = [SDS((n, model), F32), SDS((n, model), BF), SDS((2, n, units), BF), SDS((2, n, units), BF)]
    outs += [SDS((n, model), BF)] * with_term
    scratch = [pltpu.VMEM((n, model), F32)] * with_term + [pltpu.VMEM((n, 2 * attn[0].shape[1]), BF)]
    return call(order, functools.partial(mlp_fwd_body, layer), outs, scratch,
                (meta, hid, *attn, *vecs, *fc, *b_fc, *out), 3.0)


def mlp_term_body(layer, meta, act, out_own, out_sib, term):
    copy = copy_of(meta, layer, W_OUT)
    for cols in tiles(term.shape[1], 256):
        term[:, cols] = (dot_nn(act[0], out_own[copy, :, cols]) + dot_nn(act[1], out_sib[copy, :, cols])).astype(BF)


def mlp_term(order, layer, meta, act, out):
    n, model = act.shape[1], out[0].shape[2]
    return call(order, functools.partial(mlp_term_body, layer), [SDS((n, model), BF)], [], (meta, act, *out), 1.2)[0]


def entry_body(count, meta, *refs):
    hid, gm, own, other, gain_ref = refs[:5]
    prev, (grad, sums) = refs[5:5 + count], refs[5 + count:]
    back, gain, shift = norm_back(hid[...].astype(F32), vector(gain_ref, meta, 0, LN1_GAIN), pair_sum(own[...], other[...]))
    grad[...] = gm[...] + back
    found = jnp.concatenate([gain, shift], axis=0)
    sums[0:2, :] = found + prev[0][0:2, :] if count else found


def entry(order, meta, ins, prev):
    outs = [SDS(ins[0].shape, F32), SDS((8, ins[0].shape[1]), F32)]
    return call(order, functools.partial(entry_body, len(prev)), outs, [], (meta, *ins, *prev), 1.2)


def mlp_back_body(layer, count, meta, *refs):
    if layer == 1:
        g_ref, *refs = refs
        g = g_ref[...].astype(F32)
        rows = []
    else:
        hid, gm, own, other, above, *refs = refs
        back, gain, shift = norm_back(hid[...], vector(above, meta, 1, LN1_GAIN), pair_sum(own[...], other[...]))
        g = gm[...] + back
        rows = [gain, shift]
    slope, fc_own, fc_sib, out_own, out_sib, *refs = refs
    prev, refs = refs[:count], refs[count:]
    if layer == 0:
        grad, *refs = refs
        grad[...] = g
    low, gb, term, sums, bsum, acc = refs
    low[...] = g.astype(BF)
    found = jnp.concatenate([jnp.sum(g, axis=0, keepdims=True)] + rows, axis=0)
    k = found.shape[0]
    sums[0:k, :] = found + prev[0][0:k, :] if count else found
    c_fc, c_out = copy_of(meta, layer, W_FC), copy_of(meta, layer, W_OUT)
    for side, (fc, out) in enumerate(((fc_own, out_own), (fc_sib, out_sib))):
        for at, cols in enumerate(tiles(fc.shape[2], 256)):
            before = (dot_nt(low[...], out[c_out, cols, :]) * slope[side, :, cols].astype(F32)).astype(BF)
            gb[side, :, cols] = before
            total = jnp.sum(before.astype(F32), axis=0, keepdims=True)
            bsum[side:side + 1, cols] = total + prev[1][side:side + 1, cols] if count else total
            part = dot_nt(before, fc[c_fc, :, cols])
            if side == 0 and at == 0:
                acc[...] = part
            else:
                acc[...] += part
    term[...] = acc[...].astype(BF)


def mlp_back(order, layer, meta, ins, slope, fc, out, prev):
    n, model = ins[0].shape
    units = fc[0].shape[2]
    outs = [SDS((n, model), F32)] * (1 - layer) + [
        SDS((n, model), BF), SDS((2, n, units), BF), SDS((n, model), BF), SDS((8, model), F32), SDS((2, units), F32)]
    return call(order, functools.partial(mlp_back_body, layer, len(prev)), outs, [pltpu.VMEM((n, model), F32)],
                (meta, *ins, slope, *fc, *out, *prev), 2.5)


def attn_back_body(layer, stream, meta, g_ref, mid, own, other, gain_ref, q_ref, ctx, lse, w, *refs):
    count = (2, 4)[stream]
    kvs, refs = refs[:count], refs[count:]
    prev, before, refs = (refs[:1], refs[1:3], refs[3:]) if stream == 0 else ((), (), refs)
    gm, low, sums, dq = refs[:4]
    dkvs = refs[4:]
    core = meta[CORE]
    back, gain, shift = norm_back(mid[...], vector(gain_ref, meta, layer, LN2_GAIN), pair_sum(own[...], other[...]))
    g = g_ref[...].astype(F32) + back
    gm[...] = g
    low[...] = g.astype(BF)
    found = jnp.concatenate([gain, shift, jnp.sum(g, axis=0, keepdims=True)], axis=0)
    sums[0:3, :] = found + prev[0][0:3, :] if prev else found
    lane = lax.broadcasted_iota(jnp.int32, (8, LANES), 1)
    which = lax.broadcasted_iota(jnp.int32, (8, LANES), 0)
    pick = ((lane >= which * HEAD) & (lane < (which + 1) * HEAD)).astype(F32)

    def pair(j, lanes):
        gctx = dot_nt(low[...], w[lanes, :]).astype(BF)
        prod = gctx.astype(F32) * ctx[:, lanes].astype(F32)
        delta = lax.dot_general(pick, prod, (((1,), (1,)), ((), ())), precision=lax.Precision.HIGHEST,
                                preferred_element_type=F32)
        masks = head_masks()
        qhs = [jnp.where(mask, q_ref[:, lanes], BF(0)) for mask in masks]
        ghs = [jnp.where(mask, gctx, BF(0)) for mask in masks]
        dqt = [0.0, 0.0]
        for i, kv in enumerate(kvs):
            k, v = kv[0, :, lanes], kv[1, :, lanes]
            kt = jnp.transpose(k)
            dk = dv = 0.0
            for h in (0, 1):
                s = mask_scores(stream, i, dot_nt(k, qhs[h]), core)
                p = jnp.exp(s - lse[j, h:h + 1, :])
                ds = (p * (dot_nt(v, ghs[h]) - delta[h:h + 1, :])).astype(BF)
                dv = dv + dot_nn(p.astype(BF), ghs[h])
                dk = dk + dot_nn(ds, qhs[h])
                dqt[h] = dqt[h] + dot_nn(kt[h * HEAD:(h + 1) * HEAD], ds)
            if before:
                dk, dv = dk + before[i][0, :, lanes], dv + before[i][1, :, lanes]
            dkvs[i][0, :, lanes] = dk.astype(dkvs[i].dtype)
            dkvs[i][1, :, lanes] = dv.astype(dkvs[i].dtype)
        dq[:, lanes] = (jnp.transpose(jnp.concatenate(dqt, axis=0)) * HEAD ** -0.5).astype(BF)

    pair_loop(q_ref.shape[1], pair)


def attn_back(order, layer, stream, meta, grad, mid, own, other, gain, q, ctx, lse, kvs, proj, prev, before):
    n, width = q.shape
    model = mid.shape[1]
    kinds = [F32, BF] if stream == 0 else [F32, F32, F32, BF]
    outs = [SDS((n, model), F32), SDS((n, model), BF), SDS((8, model), F32), SDS((n, width), BF)]
    outs += [SDS((2, n, width), kind) for kind in kinds]
    return call(order, functools.partial(attn_back_body, layer, stream), outs, [],
                (meta, grad, mid, own, other, gain, q, ctx, lse, proj, *kvs, *prev, *before),
                (6.0, 8.6)[stream])


def attn_out_body(count, meta, dq, own, recv, w, *refs):
    prev, (joint, sums, term) = refs[:count], refs[count:]
    joint[0] = dq[...]
    joint[1] = pair_sum(own[0], recv[0]).astype(BF)
    joint[2] = pair_sum(own[1], recv[1]).astype(BF)
    for i in range(3):
        total = jnp.sum(joint[i].astype(F32), axis=0, keepdims=True)
        sums[i:i + 1, :] = total + prev[0][i:i + 1, :] if count else total
    for cols in tiles(term.shape[1], 256):
        term[:, cols] = sum(dot_nn(joint[i], w[i, :, cols]) for i in range(3)).astype(BF)


def attn_out(order, meta, dq, own, recv, w, prev):
    n, width = dq.shape
    model = w.shape[2]
    outs = [SDS((3, n, width), BF), SDS((8, width), F32), SDS((n, model), BF)]
    return call(order, functools.partial(attn_out_body, len(prev)), outs, [], (meta, dq, own, recv, w, *prev), 1.4)


def store_rows(refs, cols, value):
    at = 0
    for ref in refs:
        ref[:, cols] = value[at:at + ref.shape[0]]
        at += ref.shape[0]


def mlp_weights_body(meta, mix_a, mix_b, low_a, low_b, gb_a, gb_b, act_a, act_b, own, *refs):
    sib, left = refs[:-1], refs[-1]
    n = mix_a.shape[0]
    units = gb_a.shape[2]
    for kind, (one, two, a, b) in enumerate(((mix_a, mix_b, gb_a, gb_b), (low_a, low_b, act_a, act_b))):
        left[kind, :, :n] = jnp.transpose(one[...])
        left[kind, :, n:] = jnp.transpose(two[...])
        for side, to in ((1, sib), (0, [own])):
            for cols in tiles(units, 256):
                found = dot_nn(left[kind, :, :n], a[side, :, cols]) + dot_nn(left[kind, :, n:], b[side, :, cols])
                store_rows(to, slice(kind * units + cols.start, kind * units + cols.stop), found.astype(BF))


def mlp_weight_grads(order, meta, mixed, lows, gbs, acts):
    n, model = mixed[0].shape
    units = gbs[0].shape[2]
    outs = [SDS((model, 2 * units), BF)] + [SDS((model // CHUNKS, 2 * units), BF)] * CHUNKS
    return call(order, mlp_weights_body, outs, [pltpu.VMEM((2, model, 2 * n), BF)],
                (meta, *mixed, *lows, *gbs, *acts), 3.6)


def attn_weights_body(meta, nrm_a, nrm_b, low_a, low_b, joint_a, joint_b, ctx_a, ctx_b, own, *refs):
    sib, (left, right) = refs[:-2], refs[-2:]
    n, model = nrm_a.shape
    width = ctx_a.shape[1]
    half = width // 2
    core = meta[CORE]
    for s, (joint, ctx) in enumerate(((joint_a, ctx_a), (joint_b, ctx_b))):
        for i in range(4):
            d = joint[i] if i < 3 else ctx[...]
            lo, hi = d[:, :half], d[:, half:]
            right[0, s * n:(s + 1) * n, i * half:(i + 1) * half] = jnp.where(core == 0, lo, hi)
            right[1, s * n:(s + 1) * n, i * half:(i + 1) * half] = jnp.where(core == 0, hi, lo)
    left[0, :, :n] = jnp.transpose(nrm_a[...])
    left[0, :, n:] = jnp.transpose(nrm_b[...])
    left[1, :, :n] = jnp.transpose(low_a[...])
    left[1, :, n:] = jnp.transpose(low_b[...])
    edge = 3 * half // LANES * LANES
    for side, to in ((1, sib), (0, [own])):
        for cols in tiles(edge, 256):
            store_rows(to, cols, dot_nn(left[0], right[side, :, cols]).astype(BF))
        rest = right[side, :, edge:]
        lane = lax.broadcasted_iota(jnp.int32, (1, rest.shape[1]), 1)
        found = jnp.where(lane < 3 * half - edge, dot_nn(left[0], rest), dot_nn(left[1], rest))
        store_rows(to, slice(edge, 4 * half), found.astype(BF))


def attn_weight_grads(order, meta, normed, lows, joints, ctxs):
    n, model = normed[0].shape
    width = ctxs[0].shape[1]
    outs = [SDS((model, 2 * width), BF)] + [SDS((model // CHUNKS, 2 * width), BF)] * CHUNKS
    return call(order, attn_weights_body, outs,
                [pltpu.VMEM((2, model, 2 * n), BF), pltpu.VMEM((2, 2 * n, 2 * width), BF)],
                (meta, *normed, *lows, *joints, *ctxs), 3.2)


def pack_body(meta, ln1, *refs):
    per, (keep, send) = (refs[:4], refs[4:8]), refs[8:]
    core = meta[CORE]
    keep[...] = jnp.zeros_like(keep)
    send[...] = jnp.zeros_like(send)
    for layer, (sums_m, sums_a, bsum, jsum) in enumerate(per):
        base = 8 * layer
        first = ln1[0:2, :] if layer == 0 else per[0][0][1:3, :]
        rows = jnp.concatenate([first, sums_a[2:3, :], sums_a[0:2, :], sums_m[0:1, :]], axis=0)
        half = jsum.shape[1] // 2
        for ref, side in ((keep, 0), (send, 1)):
            ref[base:base + 6, :] = rows
            ref[base + 6:base + 7, :bsum.shape[1]] = bsum[side:side + 1, :]
            for at, i in enumerate((0, 2)):
                lo, hi = jsum[i:i + 1, :half], jsum[i:i + 1, half:]
                ref[base + 7:base + 8, at * half:(at + 1) * half] = (
                    jnp.where(core == side, lo, hi))


def pack(order, meta, ln1, parts, model):
    outs = [SDS((16, model), F32)] * 2
    return call(order, pack_body, outs, [], (meta, ln1, *parts[0], *parts[1]), 0.7)


def small_final_body(n_dp, half, units, meta, vecs, *outs):
    model = vecs.shape[1]
    place = meta[PLACE]

    def columns(width, start):
        share = width // n_dp
        turned = pltpu.roll(vecs[...], (model - start - place * share) % model, 1)
        return turned[:, :share]

    mine, units_mine = columns(model, 0), columns(units, 0)
    queries, values = columns(half, 0), columns(half, half)
    for i, (ref, index) in enumerate(zip(outs, (LN1_GAIN, LN1_SHIFT, B_PROJ, LN2_GAIN, LN2_SHIFT, B_OUT, B_FC))):
        source = units_mine if i == 6 else mine
        one, two = source[i:i + 1], source[8 + i:9 + i]
        ref[0:1, :] = jnp.where(meta[index] == 1, one + two, one)
        ref[1:2, :] = jnp.where(meta[index] == 1, jnp.zeros_like(two), two)
    for j, source in enumerate((queries, values)):
        one, two = source[7:8], source[15:16]
        outs[7][0, j:j + 1, :] = jnp.where(meta[B_QV] == 1, one + two, one)
        outs[7][1, j:j + 1, :] = jnp.where(meta[B_QV] == 1, jnp.zeros_like(two), two)


def small_final(order, meta, vecs, n_dp, half, units):
    model = vecs.shape[1]
    outs = [SDS((2, model // n_dp), F32)] * 6 + [SDS((2, units // n_dp), F32), SDS((2, 2, half // n_dp), F32)]
    return call(order, functools.partial(small_final_body, n_dp, half, units), outs, [], (meta, vecs), 1.0, keep=False)


def sib(v):
    return lax.ppermute(v, "tensor", [(0, 1), (1, 0), (2, 3), (3, 2)])


def across(v):
    return lax.ppermute(v, "tensor", [(0, 2), (2, 0), (1, 3), (3, 1)])


def part_index(bits, done, current, meta):
    mine = lambda bit: (meta[PLACE] >> bit) & 1
    return tuple(mine(b) if b in done else 1 - mine(b) if b == current else slice(None) for b in bits)


def part_sum(refs, kinds, done, current, meta):
    return sum(ref[part_index(bits, done, current, meta)].astype(F32) for ref, bits in zip(refs, kinds))


def send_body(kinds, done, current, meta, *refs):
    refs, (send, keep) = refs[:-2], refs[-2:]
    send[...] = part_sum(refs, kinds, done, current, meta).astype(BF)
    keep[...] = part_sum(refs, kinds, done + [current], None, meta).astype(BF)


def first_send_body(axis, meta, own, *refs):
    pieces, (send, keep) = refs[:-2], refs[-2:]
    bit = (meta[PLACE] >> axis) & 1
    for i, piece in enumerate(pieces):
        for ref, side in ((send, 1 - bit), (keep, bit)):
            ref[i] = (own[i, :, side].astype(F32) + piece[:, side].astype(F32)).astype(BF)


class Scatter:
    def __init__(self, own, *pieces, n_dp):
        self.n = n_dp
        self.bits, self.done = list(range(max(n_dp.bit_length() - 1, 0))), []
        self.power = n_dp == 1 << len(self.bits) and n_dp % (2 * CHUNKS) == 0
        self.own, self.pieces = own, [sib(p) for p in pieces]
        self.rows = own.shape[0] // n_dp
        self.cols = own.shape[1]
        self.kinds, self.parts = [], []

    def step(self, order, meta):
        if not self.power or not self.bits:
            return
        bit = self.bits.pop(0)
        left = tuple(self.bits)[::-1]
        if bit == 0:
            wide = self.n // CHUNKS // 2
            outs = [SDS((CHUNKS, wide, self.rows, self.cols), BF)] * 2
            send, keep = call(order, functools.partial(first_send_body, bit), outs, [],
                              (meta, self.own.reshape(CHUNKS, wide, 2, self.rows, self.cols),
                               *[p.reshape(wide, 2, self.rows, self.cols) for p in self.pieces]), 1.0)
            shape = (2,) * len(left) + (self.rows, self.cols)
            self.kinds, self.parts = [left], [keep.reshape(shape)]
            send = send.reshape(shape)
        else:
            shape = (2,) * len(left) + (self.rows, self.cols)
            send, keep = call(order, functools.partial(send_body, self.kinds, list(self.done), bit), [SDS(shape, BF)] * 2,
                              [], (meta, *self.parts), 1.0)
            self.kinds, self.parts = [left], [keep]
        self.done.append(bit)
        self.kinds = self.kinds + [left]
        self.parts = self.parts + [lax.ppermute(send, "dp", [(i, i ^ (1 << bit)) for i in range(self.n)])]

    def whole(self):
        total = pair_sum(self.own, jnp.concatenate(self.pieces))
        total = lax.psum_scatter(total, "dp", scatter_dimension=0, tiled=True)
        self.parts, self.kinds = [total], [()]


def share(ref, one, two, tied):
    ref[0] = jnp.where(tied, one + two, one)
    ref[1] = jnp.where(tied, jnp.zeros_like(two), two)


def mlp_final_body(kinds, done, meta, *refs):
    refs, (fc, out) = refs[:-2], refs[-2:]
    count = len(kinds[0])
    one = part_sum(refs[:count], kinds[0], done, None, meta)
    two = part_sum(refs[count:], kinds[1], done, None, meta)
    units = fc.shape[2]
    share(fc, one[:, :units], two[:, :units], meta[W_FC] == 1)
    share(out, one[:, units:], two[:, units:], meta[W_OUT] == 1)


def attn_final_body(kinds, done, meta, *refs):
    refs, (qkv, proj) = refs[:-2], refs[-2:]
    count = len(kinds[0])
    one = part_sum(refs[:count], kinds[0], done, None, meta)
    two = part_sum(refs[count:], kinds[1], done, None, meta)
    half = qkv.shape[3]
    tied = meta[W_QKV] == 1
    for i in range(3):
        a, b = one[:, i * half:(i + 1) * half], two[:, i * half:(i + 1) * half]
        qkv[0, i] = jnp.where(tied, a + b, a)
        qkv[1, i] = jnp.where(tied, jnp.zeros_like(b), b)
    share(proj, one[:, 3 * half:], two[:, 3 * half:], meta[W_PROJ] == 1)


def final(order, meta, body, jobs, shapes):
    for job in jobs:
        if not job.power:
            job.whole()
    kinds = [job.kinds for job in jobs]
    return call(order, functools.partial(body, kinds, jobs[0].done), [SDS(v, F32) for v in shapes], [],
                (meta, *jobs[0].parts, *jobs[1].parts), 1.0, keep=False)


def finish_body(meta, *refs):
    b_out, outs = refs[6], refs[7:]
    for s, out in enumerate(outs):
        mid, own, other = refs[3 * s:3 * s + 3]
        out[...] = (mid[...] + pair_sum(own[...], other[...]) + vector(b_out, meta, 1, B_OUT)).astype(BF)


def finish_rows(order, meta, parts, b_out):
    outs = [SDS(p[0].shape, BF) for p in parts]
    return call(order, finish_body, outs, [], (meta, *parts[0], *parts[1], b_out), 0.8)


def add_body(meta, one, two, out):
    out[...] = one[...] + two[...]


def add(order, meta, one, two):
    return call(order, add_body, [SDS(one.shape, F32)], [], (meta, one, two), 0.4)[0]


def build(n_dp):
    bits = max(n_dp.bit_length() - 1, 0)

    def per_device(tokens, cotangent, tie, ln1_gain, ln1_shift, w_qkv, b_qv, w_proj, b_proj,
                   ln2_gain, ln2_shift, w_fc, b_fc, w_out, b_out):
        core = lax.axis_index("tensor") % 2
        _, length, model = tokens.shape
        n = length // 4
        starts = (core * n, (3 - core) * n)
        meta = jnp.concatenate([tie, core[None], lax.axis_index("dp")[None], (lax.axis_index("tensor") // 2)[None], jnp.zeros_like(tie[:1])])

        order = Order()
        vectors = (b_proj, ln2_gain, ln2_shift)
        w_t = jnp.transpose(w_qkv, (0, 2, 3, 1))
        qkv, bqv = (w_t, sib(w_t)), (b_qv, sib(b_qv))
        proj = (w_proj, sib(w_proj))
        proj_far = [across(w_proj[i]) for i in (0, 1)]
        proj_far = (proj_far, [sib(v) for v in proj_far])

        rows_of = lambda v, s: lax.dynamic_slice_in_dim(v[0], starts[s], n, 0)
        recs = [[dict(), dict()], [dict(), dict()]]
        heads = [None, None]

        def fwd_in(layer, s, ins):
            r = recs[layer][s]
            *hid, r["normed"], r["q"], r["kv"] = attn_in(
                order, layer, meta, ins, ln1_gain, ln1_shift, heads[layer][0], bqv)
            r["hidden"] = hid[0] if hid else ins[0]
            r["kv_sib"] = sib(r["kv"])

        def fwd_attn(layer, s):
            r, a = recs[layer][s], recs[layer][0]
            r["kvs"] = [r["kv"], r["kv_sib"]] if s == 0 else [r["kv"], a["kv"], a["kv_sib"], r["kv_sib"]]
            r["ctx"], r["lse"] = attn_fwd(order, s, meta, r["q"], r["kvs"])
            r["attn"] = (r["ctx"], across(r["ctx"]))

        def fwd_mlp(layer, s):
            r = recs[layer][s]
            r["mid"], r["mixed"], r["act"], r["slope"], *term = mlp_fwd(
                order, layer, meta, r["hidden"], (*r["attn"], wholes[layer]), vectors, fc, bfc, out, layer == 0)
            if term:
                r["mlp"] = (term[0], across(term[0]))

        heads[0] = prep(order, 0, meta, qkv, proj)
        fwd_in(0, 0, (rows_of(tokens, 0),))
        order.waits.append(proj_far[0][0])
        fwd_in(0, 1, (rows_of(tokens, 1),))
        w_fc_late, w_out_late, *_ = lax.optimization_barrier((w_fc, w_out, recs[0][0]["kv_sib"], recs[0][1]["kv_sib"]))
        fwd_attn(0, 0)
        fc, bfc = (w_fc, sib(w_fc_late)), (b_fc, sib(b_fc))
        out = (w_out, sib(w_out_late))
        fwd_attn(0, 1)
        wholes = [prep_whole(order, 0, meta, proj, proj_far)]
        for s in (0, 1):
            fwd_mlp(0, s)
        heads[1] = prep(order, 1, meta, qkv, proj)
        wholes.append(prep_whole(order, 1, meta, proj, proj_far))
        for s in (0, 1):
            r = recs[0][s]
            fwd_in(1, s, (r["mid"], *r["mlp"], b_out))
            fwd_attn(1, s)

        back = [[dict(), dict()], [dict(), dict()]]
        sums_m, sums_a, sums_j = [(), ()], [(), ()], [(), ()]
        jobs = [[None, None], [None, None]]

        def back_mlp(layer, s, ins):
            b = back[layer][s]
            *grad, b["low"], b["gb"], term, b_sums, b_units = mlp_back(
                order, layer, meta, ins, recs[layer][s]["slope"], fc, out, sums_m[layer])
            sums_m[layer] = (b_sums, b_units)
            b["grad"] = grad[0] if grad else b["low"]
            b["mixed_term"] = (term, across(term))

        def back_mlp_weights(layer):
            rec, b = recs[layer], back[layer]
            found = mlp_weight_grads(order, meta, [r["mixed"] for r in rec], [v["low"] for v in b], [v["gb"] for v in b],
                                     [r["act"] for r in rec])
            jobs[layer][0] = Scatter(*found, n_dp=n_dp)

        def back_attn(layer, s):
            r, b = recs[layer][s], back[layer][s]
            before = back[layer][1]["to_first"] if s == 0 else ()
            b["gm"], b["low2"], sums, b["dq"], b["dkv"], *rest = attn_back(
                order, layer, s, meta, b["grad"], r["mid"], *b["mixed_term"], ln2_gain, r["q"], r["ctx"], r["lse"],
                r["kvs"], heads[layer][1], sums_a[layer], before)
            sums_a[layer] = (sums,)
            b["to_first"] = rest[:2]
            b["dkv_sib"] = sib(rest[-1])

        def back_out(layer, s):
            b = back[layer][s]
            b["joint"], sums, term = attn_out(
                order, meta, b["dq"], b["dkv"], b["dkv_sib"], heads[layer][0], sums_j[layer])
            sums_j[layer] = (sums,)
            b["ins"] = (recs[layer][s]["hidden"], b["gm"], term, across(term), ln1_gain)

        def back_attn_weights(layer):
            rec, b = recs[layer], back[layer]
            found = attn_weight_grads(order, meta, [r["normed"] for r in rec], [v["low2"] for v in b],
                                      [v["joint"] for v in b], [r["ctx"] for r in rec])
            jobs[layer][1] = Scatter(*found, n_dp=n_dp)

        def send(layer, which):
            jobs[layer][which].step(order, meta)

        finish = [None, None]

        def last_term(s):
            term = mlp_term(order, 1, meta, recs[1][s]["act"], out)
            finish[s] = (recs[1][s]["mid"], term, across(term))

        def wait(v):
            order.waits.append(v)

        for s in (0, 1):
            fwd_mlp(1, s)
            back_mlp(1, s, (rows_of(cotangent, s),))
        def received(layer, which):
            return jobs[layer][which].parts[-1] if jobs[layer][which].parts else meta

        wait(back[1][0]["mixed_term"][1])
        back_mlp_weights(1)
        back_attn(1, 1)
        send(1, 0)
        back_out(1, 1)
        back_attn(1, 0)
        wait(back[1][1]["ins"][3])
        last_term(0)
        back_out(1, 0)
        back_mlp(0, 1, back[1][1]["ins"])
        back_attn_weights(1)
        back_mlp(0, 0, back[1][0]["ins"])
        send(1, 0)
        back_mlp_weights(0)
        send(1, 1)
        back_attn(0, 1)
        send(0, 0)
        send(1, 0)
        back_out(0, 1)
        back_attn(0, 0)
        wait(back[0][1]["ins"][3])
        send(1, 1)
        back_out(0, 0)
        back_attn_weights(0)
        prev, grad = (), [0, 0]

        def last_entry(s, prev):
            grad[s], ln1 = entry(order, meta, back[0][s]["ins"], prev)
            return (ln1,)

        prev = last_entry(1, prev)
        prev = last_entry(0, prev)
        ln1 = prev[0]
        small = [(sums_m[i][0], sums_a[i][0], sums_m[i][1], sums_j[i][0]) for i in (0, 1)]
        last_term(1)
        keep, other = pack(order, meta, ln1, small, model)
        wait(received(1, 0))
        send(0, 0)
        send(0, 1)
        vecs = add(order, meta, keep, sib(other))
        rows = model // n_dp
        hid = w_fc.shape[2]
        half = w_proj.shape[1]
        power = n_dp & (n_dp - 1) == 0
        if not power:
            vecs = lax.psum(vecs, "dp")

        def exchanged(v, bit):
            return lax.ppermute(v, "dp", [(i, i ^ (1 << bit)) for i in range(n_dp)])

        rounds = bits if power else 0
        for bit in range(rounds):
            other = exchanged(vecs, bit)
            send(0, 1)
            send(0, 0)
            send(1, 1)
            if bit + 1 < rounds:
                vecs = add(order, meta, vecs, other)
        for _ in range(bits):
            send(0, 1)
            send(0, 0)
            send(1, 1)
            send(1, 0)
        result = finish_rows(order, meta, finish, b_out)
        g_fc, g_out = final(order, meta, mlp_final_body, [jobs[0][0], jobs[1][0]], [(2, rows, hid)] * 2)
        g_qkv, g_proj = final(order, meta, attn_final_body, [jobs[0][1], jobs[1][1]],
                              [(2, 3, rows, half), (2, rows, half)])
        if rounds:
            vecs = add(order, meta, vecs, other)
        small_outs = small_final(order, meta, vecs, n_dp, half, hid)
        def assemble(pieces):
            other = [sib(p) for p in pieces]
            low = jnp.where(core == 0, pieces[0], other[0]), jnp.where(core == 0, other[0], pieces[0])
            high = jnp.where(core == 0, other[1], pieces[1]), jnp.where(core == 0, pieces[1], other[1])
            return jnp.concatenate([low[0], low[1], high[0], high[1]], axis=0)[None]

        output = assemble(result)

        finals = (
            small_outs[0], small_outs[1], jnp.transpose(g_qkv, (0, 2, 1, 3)), small_outs[7],
            jnp.transpose(g_proj, (0, 2, 1)), small_outs[2], small_outs[3], small_outs[4], g_fc, small_outs[6],
            jnp.transpose(g_out, (0, 2, 1)), small_outs[5])
        return (output, assemble(grad)) + finals

    return per_device


def solution(mesh):
    return jax.shard_map(
        build(mesh.shape["dp"]),
        mesh=mesh,
        in_specs=(
            P("dp", None, None),
            P("dp", None, None),
            P(),
            P(),
            P(),
            P(None, None, None, "tensor"),
            P(None, None, "tensor"),
            P(None, "tensor", None),
            P(),
            P(),
            P(),
            P(None, None, "tensor"),
            P(None, "tensor"),
            P(None, "tensor", None),
            P(),
        ),
        out_specs=(
            P("dp", None, None),
            P("dp", None, None),
            P(None, "dp"),
            P(None, "dp"),
            P(None, "dp", None, "tensor"),
            P(None, None, ("tensor", "dp")),
            P(None, "tensor", "dp"),
            P(None, "dp"),
            P(None, "dp"),
            P(None, "dp"),
            P(None, "dp", "tensor"),
            P(None, ("tensor", "dp")),
            P(None, "tensor", "dp"),
            P(None, "dp"),
        ),
        check_vma=False,
    )
```
